32 devices in a mesh: grp: 2 (over x), exp: 16 (over z, y, core).
Axes of the slice: x: 2, y: 2, z: 4, core: 2. Of those that a mesh axis runs over, the one named last changes fastest.
Arguments:
- tokens: bfloat16 [512, 2048], P(('grp', 'exp')), parts along dimension 0, may hold values from -6 to 6
- router_weight: bfloat16 [2048, 16], replicated, may hold values from -0.0625 to 0.0625
- w_gate: bfloat16 [16, 2048, 768], P('exp'), may hold values from -0.125 to 0.125
- w_up: bfloat16 [16, 2048, 768], P('exp'), may hold values from -0.125 to 0.125
- w_down: bfloat16 [16, 768, 2048], P('exp'), may hold values from -0.3125 to 0.3125
- expert_ids: int32 [512, 8], P(('grp', 'exp')), parts along dimension 0, may hold values from 0 to 15, all different within a row; in each aligned block of 16 rows (0 to 15, 16 to 31, ...) at most 12 rows name the same one
Outputs:
- moe_out: bfloat16 [512, 2048], P(('grp', 'exp')), parts along dimension 0
The draws below stay inside these ranges and needn't reach their ends.
There are 2 independent parts, one for each index of `grp`. The reference program is written for one: setup_inputs(seed, part) draws one part's arguments, and reference() takes and returns one part's arrays. A program takes and returns all parts, laid end to end along the dimension named above; an argument that names none is the same for every part. Nothing has to cross between parts.
Inputs may be any that keep to these rules, and one draw needn't show every extreme that they name: `expert_ids`: each row names 8 different experts; among the 16 rows of one device no expert is named by more than 12 rows.
All inputs are finite; a program needn't handle non-finite values.
Results may differ from the reference program's by a relative error of at most 0.0085.
Values may be sent and summed in bfloat16 or wider, within the bound.
A program may use at most 64 MiB of HBM per device.

```python
import math
import jax
import jax.numpy as jnp
import numpy as np
from jax import lax

D = 2048
FF = 768
TOP = 8
TOK_DEV = 16
EXPERTS = 16
TOKENS = 256
CAP = 12
N_EXP = 16


def steps_of(own_key, dims, pieces, low, largest):
    def one(dim, blocks):
        draws = jax.random.uniform(jax.random.fold_in(jax.random.fold_in(own_key, 6), dim), (blocks,), jnp.float32, low / len(pieces), largest / len(pieces))
        return jnp.repeat(jnp.exp(draws), dims[dim] // blocks).reshape((-1,) + (1,) * (len(dims) - dim - 1))

    level = one(*pieces[0])
    for cut in pieces[1:]:
        level = level * one(*cut)
    return level


def deal_out(own_key, own, number, rows, number_of, top, limit, skew):
    order = jax.random.permutation(own_key, number_of)
    heavy_load, ordinary = load_shares(number_of, rows * top, limit, skew, True), load_shares(number_of, rows * top, limit, skew, False)
    places = jnp.arange(number_of)

    def named(tallies, rotation):
        used = int((tallies > 0).sum())
        fixed = max(1, used // 4)
        passed = fixed + (places - fixed + rotation * (used - fixed)) % max(1, number_of - fixed)
        return jnp.zeros((number_of,), jnp.int32).at[order[jnp.where(places < fixed, places, passed)]].set(jnp.asarray(tallies, jnp.int32))

    tallies = jnp.where(number % 4 == 0, named(heavy_load, number // 4), named(ordinary, number - number // 4 - 1))
    mixed = jax.random.permutation(jax.random.fold_in(own, 3), number_of)
    giver, receiver = mixed[0:number_of // 2 * 2:2], mixed[1:number_of // 2 * 2:2]
    margin = jnp.minimum(tallies[giver] - 1, limit - tallies[receiver]) // 2
    margin = jnp.where((giver == order[0]) | (receiver == order[0]) | (tallies[receiver] == 0), 0, jnp.maximum(margin, 0))
    passed = jax.random.randint(jax.random.fold_in(own, 4), (number_of // 2,), 0, 1 << 20) % (margin + 1)
    tallies = tallies.at[giver].add(-passed).at[receiver].add(passed)
    members = jnp.searchsorted(jnp.cumsum(tallies), jnp.arange(rows * top), side="right").astype(jnp.int32)
    listing = members.reshape(top, rows).T
    listing = listing[jax.random.permutation(jax.random.fold_in(own, 1), rows)]
    rotation = jax.random.randint(jax.random.fold_in(own, 2), (rows, 1), 0, top)
    return jnp.take_along_axis(listing, (jnp.arange(top)[None, :] + rotation) % top, axis=1)


def load_shares(count, total, reach, slope, full):
    loads = [(1 << 20) // math.isqrt(grade ** slope) + 1 for grade in range(1, count + 1)]
    largest = reach if full else min(reach, max(-(-total // count), total * loads[0] // sum(loads)))
    least = 1 if total - largest >= count - 1 else 0
    holding, spare = [largest] + [least] * (count - 1), total - largest - least * (count - 1)
    while spare > 0:
        movable = [i for i in range(1, count) if holding[i] < largest] or [i for i in range(1, count) if holding[i] < reach]
        pool, budget = sum([loads[i] for i in movable]), spare
        for i in movable:
            more = min(reach - holding[i], max(1, budget * loads[i] // pool), spare)
            holding[i] = holding[i] + more
            spare = spare - more
    return np.array(holding)


def normal_values(stream_key, dims, width, most, split=(), held_as=jnp.bfloat16):
    level = steps_of(stream_key, dims, split, -0.22, 0.18) if split else 1.0
    array = jax.random.normal(stream_key, dims, jnp.float32) * width * level
    return jnp.minimum(jnp.maximum(array, -most), most).astype(held_as)


def setup_inputs(seed: int = 0, part: int = 0) -> dict:
    key_of = jax.random.split(jax.random.key(seed), 7)
    part_keys = jax.random.split(jax.random.fold_in(key_of[6], part), 7)
    tokens = normal_values(part_keys[0], (TOKENS, D), 1.0, 6.0, ((0, 16),))
    router_weight = normal_values(key_of[1], (D, EXPERTS), (4 * D) ** -0.5, 0.0625)
    w_gate = normal_values(key_of[2], (EXPERTS, D, FF), D ** -0.5, 0.125, ((0, 16),))
    w_up = normal_values(key_of[3], (EXPERTS, D, FF), D ** -0.5, 0.125, ((0, 16),))
    w_down = normal_values(key_of[4], (EXPERTS, FF, D), (FF // 2) ** -0.5, 0.3125, ((0, 16),))
    expert_ids_keys = jax.random.split(jax.random.fold_in(part_keys[5], 1), TOKENS // TOK_DEV)
    expert_ids_turns = jax.random.permutation(jax.random.fold_in(part_keys[5], 3), TOKENS // TOK_DEV)
    expert_ids = jax.vmap(lambda own, number: deal_out(jax.random.fold_in(part_keys[5], 2), own, number, TOK_DEV, EXPERTS, TOP, CAP, 2))(expert_ids_keys, expert_ids_turns).reshape((TOKENS, TOP))
    return dict(tokens=tokens, router_weight=router_weight, w_gate=w_gate, w_up=w_up, w_down=w_down, expert_ids=expert_ids)


def expert_rows(rows, gate_mat, up_mat, down_mat):
    gate = jnp.dot(rows, gate_mat, preferred_element_type=jnp.float32)
    upper = jnp.dot(rows, up_mat, preferred_element_type=jnp.float32)
    act = (jax.nn.silu(gate) * upper).astype(jnp.bfloat16)
    return jnp.dot(act, down_mat, preferred_element_type=jnp.float32).astype(jnp.bfloat16)


def reference(tokens, router_weight, w_gate, w_up, w_down, expert_ids):
    logits = jnp.dot(tokens, router_weight, preferred_element_type=jnp.float32)
    picked = jnp.take_along_axis(logits, expert_ids, axis=1)
    gates = jax.nn.softmax(picked, axis=1)
    total_rows = N_EXP * CAP

    def step(carry, inputs):
        index, gate_mat, up_mat, down_mat = inputs
        match = (expert_ids == index)
        hit = jnp.any(match, axis=1).astype(jnp.int32)
        rank = jnp.cumsum(hit) - hit
        dest = jnp.where(hit == 1, rank, total_rows).astype(jnp.int32)
        rows = jnp.zeros((total_rows, D), jnp.bfloat16).at[dest].set(tokens, mode="drop")
        outs = expert_rows(rows, gate_mat, up_mat, down_mat)
        taken = outs[jnp.minimum(dest, total_rows - 1)].astype(jnp.float32)
        weight = jnp.sum(jnp.where(match, gates, jnp.float32(0.0)), axis=1)
        return carry + weight[:, None] * taken, None

    start = jnp.zeros(tokens.shape, jnp.float32)
    indices = jnp.arange(w_gate.shape[0], dtype=jnp.int32)
    total, _ = lax.scan(step, start, (indices, w_gate, w_up, w_down))
    return total.astype(jnp.bfloat16)
```

```python
import functools
import jax
import jax.numpy as jnp
from jax import lax
from jax.experimental import pallas as pl
from jax.experimental.pallas import tpu as pltpu
from jax.sharding import PartitionSpec as P

LANES = 128
MESH = pl.DeviceIdType.MESH


def expert_rows(rows, gate_mat, up_mat, down_mat):
    gate = jnp.dot(rows, gate_mat, preferred_element_type=jnp.float32)
    upper = jnp.dot(rows, up_mat, preferred_element_type=jnp.float32)
    act = (jax.nn.silu(gate) * upper).astype(jnp.bfloat16)
    return jnp.dot(act, down_mat, preferred_element_type=jnp.float32).astype(jnp.bfloat16)


def dispatch_plan(tokens, router_weight, w_gate, w_up, w_down, expert_ids, capacity):
    devices = lax.axis_size("exp")
    tok_rows, chosen = expert_ids.shape
    width = tokens.shape[1]
    experts = devices * w_gate.shape[0]
    logits = jnp.dot(tokens, router_weight, preferred_element_type=jnp.float32)
    picked = jnp.take_along_axis(logits, expert_ids, axis=1)
    gates = jax.nn.softmax(picked, axis=1)
    flat_ids = expert_ids.reshape(-1)
    onehot = (flat_ids[:, None] == jnp.arange(experts, dtype=jnp.int32)[None, :]).astype(jnp.int32)
    ranks = jnp.cumsum(onehot, axis=0) - onehot
    slot = jnp.sum(ranks * onehot, axis=1)
    place = slot * experts + flat_ids
    repeated = jnp.repeat(tokens, chosen, axis=0)
    filled = jnp.zeros((capacity * experts, width), jnp.bfloat16).at[place].set(repeated)
    received = lax.all_to_all(
        filled.reshape(capacity, experts, width), "exp", split_axis=1, concat_axis=1, tiled=True
    )
    count = received.shape[0]
    outs = expert_rows(received.reshape(-1, width), w_gate[0], w_up[0], w_down[0])
    back = lax.all_to_all(
        outs.reshape(count, experts, width), "exp", split_axis=1, concat_axis=1, tiled=True
    )
    values = back.reshape(capacity * experts, width)[place].reshape(tok_rows, chosen, width)
    mixed = jnp.einsum("tk,tkd->td", gates, values.astype(jnp.float32))
    return mixed.astype(jnp.bfloat16)


def moe_kernel(
    Z, Q, tok, router, ids, w_gate, w_up, w_down, out,
    rows, ids_v, router_v, gate_v, up_v, down_v, act,
    keep, core_out, core_in, y_out, y_in, z_out, z_in,
    load_sem, gz_s, gz_r, gy_s, gy_r, gc_s, gc_r,
    rc_s, rc_r, ry_s, ry_r, rz_s, rz_r,
):
    R, D = tok.shape
    experts = router.shape[0]
    ff = gate_v.shape[1]
    half, quarter = 2 * Z * R, Z * R
    cols = D // Q
    me = lax.axis_index("exp")
    core, y, z = lax.rem(me, 2), lax.rem(me // 2, 2), me // 4
    core_peer = {"exp": me + 1 - 2 * core}
    y_peer = {"exp": me + 2 - 4 * y}

    def z_peer(shift):
        return {"exp": lax.rem(z + shift, Z) * 4 + 2 * y + core}

    def remote(src, dst, send, recv, peer):
        return pltpu.make_async_remote_copy(
            src_ref=src, dst_ref=dst, send_sem=send, recv_sem=recv,
            device_id=peer, device_id_type=MESH,
        )

    def slot(i, n=1):
        return rows.at[pl.ds(i * R, n * R)]

    loads = [
        pltpu.make_async_copy(ids, ids_v, load_sem.at[0]),
        pltpu.make_async_copy(tok, rows.at[pl.ds(0, R), pl.ds(0, D)], load_sem.at[1]),
        pltpu.make_async_copy(router, router_v, load_sem.at[2]),
        pltpu.make_async_copy(w_gate.at[0], gate_v, load_sem.at[3]),
        pltpu.make_async_copy(w_up.at[0], up_v, load_sem.at[4]),
        pltpu.make_async_copy(w_down.at[0], down_v, load_sem.at[5]),
    ]
    for load in loads[:2]:
        load.start()
    barrier = pltpu.get_barrier_semaphore()
    for peer in [core_peer, y_peer] + [z_peer(s) for s in range(1, Z)]:
        pl.semaphore_signal(barrier, inc=1, device_id=peer, device_id_type=MESH)
    for load in loads[2:]:
        load.start()
    loads[0].wait()
    lane = lax.broadcasted_iota(jnp.int32, (LANES, R), 0)
    named = jnp.zeros((LANES, R), jnp.float32)
    for k in range(ids.shape[0]):
        named = jnp.where(ids_v[k : k + 1, :] == lane, 1.0, named)
    rows[0:R, D : D + LANES] = named.T.astype(jnp.bfloat16)
    loads[1].wait()
    pl.semaphore_wait(barrier, Z + 1)

    along_z = [
        remote(slot(0), slot(s), gz_s.at[s], gz_r.at[s], z_peer(Z - s)) for s in range(1, Z)
    ]
    across_y = [
        remote(slot(s), slot(Z + s), gy_s.at[s], gy_r.at[s], y_peer) for s in range(Z)
    ]
    to_core = [
        remote(slot(s), slot(2 * Z + s), gc_s.at[s], gc_r.at[s], core_peer) for s in range(2 * Z)
    ]
    order = [0] + sorted(range(1, Z), key=lambda s: min(s, Z - s))
    for s in order[1:]:
        along_z[s - 1].start()
    across_y[0].start()
    to_core[0].start()
    for s in order[1:]:
        along_z[s - 1].wait_recv()
        across_y[s].start()
        to_core[s].start()
    for s in order:
        across_y[s].wait_recv()
        to_core[Z + s].start()
    for copy in to_core:
        copy.wait_recv()

    for load in loads[2:]:
        load.wait()
    x = rows[:, 0:D]
    logits = lax.dot_general(
        x, router_v[...], (((1,), (1,)), ((), ())), preferred_element_type=jnp.float32
    )
    chosen = rows[:, D : D + experts].astype(jnp.float32) > 0.5
    top = jnp.max(jnp.where(chosen, logits, -jnp.inf), axis=1, keepdims=True)
    weight = jnp.where(chosen, jnp.exp(jnp.where(chosen, logits - top, 0.0)), 0.0)
    mine = lax.broadcasted_iota(jnp.int32, weight.shape, 1) == me
    share = jnp.sum(jnp.where(mine, weight, 0.0), axis=1, keepdims=True)
    gates = share / jnp.sum(weight, axis=1, keepdims=True)

    step = 256
    for j in range(0, ff, step):
        g = jnp.dot(rows[:, 0:D], gate_v[:, j : j + step], preferred_element_type=jnp.float32)
        u = jnp.dot(rows[:, 0:D], up_v[:, j : j + step], preferred_element_type=jnp.float32)
        act[:, j : j + step] = (g / (1.0 + jnp.exp(-g)) * u).astype(jnp.bfloat16)

    core_back = [
        remote(core_out.at[q], core_in.at[q], rc_s.at[q], rc_r.at[q], core_peer) for q in range(Q)
    ]
    y_back = [remote(y_out.at[q], y_in.at[q], ry_s.at[q], ry_r.at[q], y_peer) for q in range(Q)]
    z_back = [
        [
            remote(z_out.at[q, s - 1], z_in.at[q, s - 1], rz_s.at[q, s - 1], rz_r.at[q, s - 1], z_peer(s))
            for s in range(1, Z)
        ]
        for q in range(Q)
    ]

    def first(q):
        o = jnp.dot(act[...], down_v[:, q * cols : (q + 1) * cols], preferred_element_type=jnp.float32)
        o = o * gates
        core_out[q] = o[half:].astype(jnp.bfloat16)
        keep[q] = o[:half]
        core_back[q].start()

    def second(q):
        core_back[q].wait_recv()
        total = keep[q] + core_in[q].astype(jnp.float32)
        y_out[q] = total[quarter:].astype(jnp.bfloat16)
        keep[q, 0:quarter] = total[:quarter]
        y_back[q].start()

    def third(q):
        y_back[q].wait_recv()
        total = keep[q, 0:quarter] + y_in[q].astype(jnp.float32)
        for s in range(1, Z):
            z_out[q, s - 1] = total[s * R : (s + 1) * R].astype(jnp.bfloat16)
            z_back[q][s - 1].start()
        keep[q, 0:R] = total[:R]

    def last(q):
        total = keep[q, 0:R]
        for s in range(1, Z):
            z_back[q][s - 1].wait_recv()
            total = total + z_in[q, s - 1].astype(jnp.float32)
        out[:, q * cols : (q + 1) * cols] = total.astype(jnp.bfloat16)

    for t in range(Q + 3):
        for lag, stage in enumerate((first, second, third, last)):
            if 0 <= t - lag < Q:
                stage(t - lag)
    for copy in along_z + across_y + to_core + core_back + y_back + sum(z_back, []):
        copy.wait_send()


def gather_plan(tokens, router_weight, w_gate, w_up, w_down, expert_ids):
    devices = lax.axis_size("exp")
    R, D = tokens.shape
    Z, Q = devices // 4, 4
    experts = router_weight.shape[1]
    ff = w_gate.shape[2]
    total, half, quarter, cols = devices * R, devices * R // 2, devices * R // 4, D // Q
    bf, f32, dma = jnp.bfloat16, jnp.float32, pltpu.SemaphoreType.DMA
    return pl.pallas_call(
        functools.partial(moe_kernel, Z, Q),
        out_shape=jax.ShapeDtypeStruct((R, D), bf),
        in_specs=[pl.BlockSpec(memory_space=pl.ANY)] * 6,
        out_specs=pl.BlockSpec(memory_space=pltpu.VMEM),
        scratch_shapes=[
            pltpu.VMEM((total, D + LANES), bf),
            pltpu.VMEM(expert_ids.shape[::-1], jnp.int32),
            pltpu.VMEM((experts, D), bf),
            pltpu.VMEM((D, ff), bf),
            pltpu.VMEM((D, ff), bf),
            pltpu.VMEM((ff, D), bf),
            pltpu.VMEM((total, ff), bf),
            pltpu.VMEM((Q, half, cols), f32),
            pltpu.VMEM((Q, half, cols), bf),
            pltpu.VMEM((Q, half, cols), bf),
            pltpu.VMEM((Q, quarter, cols), bf),
            pltpu.VMEM((Q, quarter, cols), bf),
            pltpu.VMEM((Q, Z - 1, R, cols), bf),
            pltpu.VMEM((Q, Z - 1, R, cols), bf),
            dma((6,)),
            dma((Z,)), dma((Z,)), dma((Z,)), dma((Z,)), dma((2 * Z,)), dma((2 * Z,)),
            dma((Q,)), dma((Q,)), dma((Q,)), dma((Q,)), dma((Q, Z - 1)), dma((Q, Z - 1)),
        ],
        compiler_params=pltpu.CompilerParams(
            collective_id=0, has_side_effects=True, vmem_limit_bytes=48 * 1024 * 1024
        ),
    )(tokens, router_weight.T, expert_ids.T, w_gate, w_up, w_down)


def on_device(tokens, router_weight, w_gate, w_up, w_down, expert_ids):
    devices = lax.axis_size("exp")
    tok_rows, chosen = expert_ids.shape
    experts = devices * w_gate.shape[0]
    capacity = min(tok_rows, max(2, (3 * tok_rows * chosen + 2 * experts - 1) // (2 * experts)))
    args = (tokens, router_weight, w_gate, w_up, w_down, expert_ids)
    if tok_rows <= 2 * capacity:
        return gather_plan(*args)
    return dispatch_plan(*args, capacity)


def solution(mesh):
    placed = (
        P(("grp", "exp"), None),
        P(),
        P("exp", None, None),
        P("exp", None, None),
        P("exp", None, None),
        P(("grp", "exp"), None),
    )
    return jax.shard_map(
        on_device, mesh=mesh, in_specs=placed, out_specs=P(("grp", "exp"), None), check_vma=False
    )
```

```python
import functools
import jax
import jax.numpy as jnp
from jax import lax
from jax.experimental import pallas as pl
from jax.experimental.pallas import tpu as pltpu
from jax.sharding import PartitionSpec as P

LANES = 128
MESH = pl.DeviceIdType.MESH


def expert_rows(rows, gate_mat, up_mat, down_mat):
    gate = jnp.dot(rows, gate_mat, preferred_element_type=jnp.float32)
    upper = jnp.dot(rows, up_mat, preferred_element_type=jnp.float32)
    act = (jax.nn.silu(gate) * upper).astype(jnp.bfloat16)
    return jnp.dot(act, down_mat, preferred_element_type=jnp.float32).astype(jnp.bfloat16)


def dispatch_plan(tokens, router_weight, w_gate, w_up, w_down, expert_ids, capacity):
    devices = lax.axis_size("exp")
    tok_rows, chosen = expert_ids.shape
    width = tokens.shape[1]
    experts = devices * w_gate.shape[0]
    logits = jnp.dot(tokens, router_weight, preferred_element_type=jnp.float32)
    picked = jnp.take_along_axis(logits, expert_ids, axis=1)
    gates = jax.nn.softmax(picked, axis=1)
    flat_ids = expert_ids.reshape(-1)
    onehot = (flat_ids[:, None] == jnp.arange(experts, dtype=jnp.int32)[None, :]).astype(jnp.int32)
    ranks = jnp.cumsum(onehot, axis=0) - onehot
    slot = jnp.sum(ranks * onehot, axis=1)
    place = slot * experts + flat_ids
    repeated = jnp.repeat(tokens, chosen, axis=0)
    filled = jnp.zeros((capacity * experts, width), jnp.bfloat16).at[place].set(repeated)
    received = lax.all_to_all(
        filled.reshape(capacity, experts, width), "exp", split_axis=1, concat_axis=1, tiled=True
    )
    count = received.shape[0]
    outs = expert_rows(received.reshape(-1, width), w_gate[0], w_up[0], w_down[0])
    back = lax.all_to_all(
        outs.reshape(count, experts, width), "exp", split_axis=1, concat_axis=1, tiled=True
    )
    values = back.reshape(capacity * experts, width)[place].reshape(tok_rows, chosen, width)
    mixed = jnp.einsum("tk,tkd->td", gates, values.astype(jnp.float32))
    return mixed.astype(jnp.bfloat16)


def moe_kernel(
    Z, Q, G, tok, router, ids, w_gate, w_up, w_down, out,
    rows, ids_v, router_v, gate_v, up_v, down_v, act,
    keep, core_out, core_in, y_out, y_in, z_out, z_in,
    load_sem, gz_s, gz_r, gy_s, gy_r, gc_s, gc_r,
    rc_s, rc_r, ry_s, ry_r, rz_s, rz_r,
):
    R, D = tok.shape
    experts = router.shape[0]
    ff = gate_v.shape[1]
    half, quarter = 2 * Z * R, Z * R
    cols = D // Q
    me = lax.axis_index("exp")
    core, y, z = lax.rem(me, 2), lax.rem(me // 2, 2), me // 4
    core_peer = {"exp": me + 1 - 2 * core}
    y_peer = {"exp": me + 2 - 4 * y}

    def z_peer(shift):
        return {"exp": lax.rem(z + shift, Z) * 4 + 2 * y + core}

    def remote(src, dst, send, recv, peer):
        return pltpu.make_async_remote_copy(
            src_ref=src, dst_ref=dst, send_sem=send, recv_sem=recv,
            device_id=peer, device_id_type=MESH,
        )

    loads = [
        pltpu.make_async_copy(ids, ids_v, load_sem.at[0]),
        pltpu.make_async_copy(tok, rows.at[pl.ds(0, R), pl.ds(0, D)], load_sem.at[1]),
        pltpu.make_async_copy(router, router_v, load_sem.at[2]),
        pltpu.make_async_copy(w_gate.at[0], gate_v, load_sem.at[3]),
        pltpu.make_async_copy(w_up.at[0], up_v, load_sem.at[4]),
        pltpu.make_async_copy(w_down.at[0], down_v, load_sem.at[5]),
    ]
    for load in loads[:2]:
        load.start()
    barrier = pltpu.get_barrier_semaphore()
    for peer in [core_peer, y_peer] + [z_peer(s) for s in range(1, Z)]:
        pl.semaphore_signal(barrier, inc=1, device_id=peer, device_id_type=MESH)
    for load in loads[2:]:
        load.start()
    loads[0].wait()
    lane = lax.broadcasted_iota(jnp.int32, (LANES, R), 0)
    named = jnp.zeros((LANES, R), jnp.float32)
    for k in range(ids.shape[0]):
        named = jnp.where(ids_v[k : k + 1, :] == lane, 1.0, named)
    rows[0:R, D : D + LANES] = named.T.astype(jnp.bfloat16)
    loads[1].wait()
    pl.semaphore_wait(barrier, Z + 1)

    tiles = rows.shape[1] // LANES
    edges = [(tiles * g + G - 1) // G * LANES for g in range(G + 1)]

    def slots(i, n, g):
        return rows.at[pl.ds(i * R, n * R), pl.ds(edges[g], edges[g + 1] - edges[g])]

    along_z = [
        [remote(slots(0, 1, g), slots(s, 1, g), gz_s.at[g, s], gz_r.at[g, s], z_peer(Z - s)) for s in range(Z)]
        for g in range(G)
    ]
    across_y = [
        [remote(slots(s, 1, g), slots(Z + s, 1, g), gy_s.at[g, s], gy_r.at[g, s], y_peer) for s in range(Z)]
        for g in range(G)
    ]
    to_core = [
        [
            remote(slots(h * Z, Z, g), slots((2 + h) * Z, Z, g), gc_s.at[g, h], gc_r.at[g, h], core_peer)
            for h in range(2)
        ]
        for g in range(G)
    ]
    order = sorted(range(1, Z), key=lambda s: min(s, Z - s))
    for g in range(G):
        across_y[g][0].start()
        for s in order:
            along_z[g][s].start()
    for g in range(G):
        for s in order:
            along_z[g][s].wait_recv()
            across_y[g][s].start()
        to_core[g][0].start()
    for g in range(G):
        for s in [0] + order:
            across_y[g][s].wait_recv()
        to_core[g][1].start()
    for g in range(G):
        for h in range(2):
            to_core[g][h].wait_recv()

    for load in loads[2:]:
        load.wait()
    x = rows[:, 0:D]
    logits = lax.dot_general(
        x, router_v[...], (((1,), (1,)), ((), ())), preferred_element_type=jnp.float32
    )
    chosen = rows[:, D : D + experts].astype(jnp.float32) > 0.5
    top = jnp.max(jnp.where(chosen, logits, -jnp.inf), axis=1, keepdims=True)
    weight = jnp.where(chosen, jnp.exp(jnp.where(chosen, logits - top, 0.0)), 0.0)
    mine = lax.broadcasted_iota(jnp.int32, weight.shape, 1) == me
    share = jnp.sum(jnp.where(mine, weight, 0.0), axis=1, keepdims=True)
    gates = share / jnp.sum(weight, axis=1, keepdims=True)

    step = 256
    for j in range(0, ff, step):
        g = jnp.dot(rows[:, 0:D], gate_v[:, j : j + step], preferred_element_type=jnp.float32)
        u = jnp.dot(rows[:, 0:D], up_v[:, j : j + step], preferred_element_type=jnp.float32)
        act[:, j : j + step] = (g / (1.0 + jnp.exp(-g)) * u).astype(jnp.bfloat16)

    core_back = [
        remote(core_out.at[q], core_in.at[q], rc_s.at[q], rc_r.at[q], core_peer) for q in range(Q)
    ]
    y_back = [remote(y_out.at[q], y_in.at[q], ry_s.at[q], ry_r.at[q], y_peer) for q in range(Q)]
    z_back = [
        [
            remote(z_out.at[q, s - 1], z_in.at[q, s - 1], rz_s.at[q, s - 1], rz_r.at[q, s - 1], z_peer(s))
            for s in range(1, Z)
        ]
        for q in range(Q)
    ]

    def first(q):
        o = jnp.dot(act[...], down_v[:, q * cols : (q + 1) * cols], preferred_element_type=jnp.float32)
        o = o * gates
        core_out[q] = o[half:].astype(jnp.bfloat16)
        keep[q] = o[:half]
        core_back[q].start()

    def second(q):
        core_back[q].wait_recv()
        total = keep[q] + core_in[q].astype(jnp.float32)
        y_out[q] = total[quarter:].astype(jnp.bfloat16)
        keep[q, 0:quarter] = total[:quarter]
        y_back[q].start()

    def third(q):
        y_back[q].wait_recv()
        total = keep[q, 0:quarter] + y_in[q].astype(jnp.float32)
        for s in range(1, Z):
            z_out[q, s - 1] = total[s * R : (s + 1) * R].astype(jnp.bfloat16)
            z_back[q][s - 1].start()
        keep[q, 0:R] = total[:R]

    def last(q):
        total = keep[q, 0:R]
        for s in range(1, Z):
            z_back[q][s - 1].wait_recv()
            total = total + z_in[q, s - 1].astype(jnp.float32)
        out[:, q * cols : (q + 1) * cols] = total.astype(jnp.bfloat16)

    for q in range(Q + 1):
        if q < Q:
            first(q)
        if q > 0:
            second(q - 1)
    for stage in (third, last):
        for q in range(Q):
            stage(q)
    sent = [copy for g in range(G) for copy in along_z[g][1:] + across_y[g] + to_core[g]]
    for copy in sent + core_back + y_back + sum(z_back, []):
        copy.wait_send()


def gather_plan(tokens, router_weight, w_gate, w_up, w_down, expert_ids):
    devices = lax.axis_size("exp")
    R, D = tokens.shape
    Z, Q, G = devices // 4, 4, 4
    experts = router_weight.shape[1]
    ff = w_gate.shape[2]
    total, half, quarter, cols = devices * R, devices * R // 2, devices * R // 4, D // Q
    bf, f32, dma = jnp.bfloat16, jnp.float32, pltpu.SemaphoreType.DMA
    return pl.pallas_call(
        functools.partial(moe_kernel, Z, Q, G),
        out_shape=jax.ShapeDtypeStruct((R, D), bf),
        in_specs=[pl.BlockSpec(memory_space=pltpu.HBM)] * 6,
        out_specs=pl.BlockSpec(memory_space=pltpu.VMEM),
        scratch_shapes=[
            pltpu.VMEM((total, D + LANES), bf),
            pltpu.VMEM(expert_ids.shape[::-1], jnp.int32),
            pltpu.VMEM((experts, D), bf),
            pltpu.VMEM((D, ff), bf),
            pltpu.VMEM((D, ff), bf),
            pltpu.VMEM((ff, D), bf),
            pltpu.VMEM((total, ff), bf),
            pltpu.VMEM((Q, half, cols), f32),
            pltpu.VMEM((Q, half, cols), bf),
            pltpu.VMEM((Q, half, cols), bf),
            pltpu.VMEM((Q, quarter, cols), bf),
            pltpu.VMEM((Q, quarter, cols), bf),
            pltpu.VMEM((Q, Z - 1, R, cols), bf),
            pltpu.VMEM((Q, Z - 1, R, cols), bf),
            dma((6,)),
            dma((G, Z)), dma((G, Z)), dma((G, Z)), dma((G, Z)), dma((G, 2)), dma((G, 2)),
            dma((Q,)), dma((Q,)), dma((Q,)), dma((Q,)), dma((Q, Z - 1)), dma((Q, Z - 1)),
        ],
        compiler_params=pltpu.CompilerParams(
            collective_id=0, has_side_effects=True, vmem_limit_bytes=60 * 1024 * 1024
        ),
    )(tokens, router_weight.T, expert_ids.T, w_gate, w_up, w_down)


def on_device(tokens, router_weight, w_gate, w_up, w_down, expert_ids):
    devices = lax.axis_size("exp")
    tok_rows, chosen = expert_ids.shape
    experts = devices * w_gate.shape[0]
    capacity = min(tok_rows, max(2, (3 * tok_rows * chosen + 2 * experts - 1) // (2 * experts)))
    args = (tokens, router_weight, w_gate, w_up, w_down, expert_ids)
    if tok_rows <= 2 * capacity:
        return gather_plan(*args)
    return dispatch_plan(*args, capacity)


def solution(mesh):
    placed = (
        P(("grp", "exp"), None),
        P(),
        P("exp", None, None),
        P("exp", None, None),
        P("exp", None, None),
        P(("grp", "exp"), None),
    )
    return jax.shard_map(
        on_device, mesh=mesh, in_specs=placed, out_specs=P(("grp", "exp"), None), check_vma=False
    )
```

```python
import functools
import jax
import jax.numpy as jnp
from jax import lax
from jax.experimental import pallas as pl
from jax.experimental.pallas import tpu as pltpu
from jax.sharding import PartitionSpec as P

LANES = 128
MESH = pl.DeviceIdType.MESH


def expert_rows(rows, gate_mat, up_mat, down_mat):
    gate = jnp.dot(rows, gate_mat, preferred_element_type=jnp.float32)
    upper = jnp.dot(rows, up_mat, preferred_element_type=jnp.float32)
    act = (jax.nn.silu(gate) * upper).astype(jnp.bfloat16)
    return jnp.dot(act, down_mat, preferred_element_type=jnp.float32).astype(jnp.bfloat16)


def dispatch_plan(tokens, router_weight, w_gate, w_up, w_down, expert_ids, capacity):
    devices = lax.axis_size("exp")
    tok_rows, chosen = expert_ids.shape
    width = tokens.shape[1]
    experts = devices * w_gate.shape[0]
    logits = jnp.dot(tokens, router_weight, preferred_element_type=jnp.float32)
    picked = jnp.take_along_axis(logits, expert_ids, axis=1)
    gates = jax.nn.softmax(picked, axis=1)
    flat_ids = expert_ids.reshape(-1)
    onehot = (flat_ids[:, None] == jnp.arange(experts, dtype=jnp.int32)[None, :]).astype(jnp.int32)
    ranks = jnp.cumsum(onehot, axis=0) - onehot
    slot = jnp.sum(ranks * onehot, axis=1)
    place = slot * experts + flat_ids
    repeated = jnp.repeat(tokens, chosen, axis=0)
    filled = jnp.zeros((capacity * experts, width), jnp.bfloat16).at[place].set(repeated)
    received = lax.all_to_all(
        filled.reshape(capacity, experts, width), "exp", split_axis=1, concat_axis=1, tiled=True
    )
    count = received.shape[0]
    outs = expert_rows(received.reshape(-1, width), w_gate[0], w_up[0], w_down[0])
    back = lax.all_to_all(
        outs.reshape(count, experts, width), "exp", split_axis=1, concat_axis=1, tiled=True
    )
    values = back.reshape(capacity * experts, width)[place].reshape(tok_rows, chosen, width)
    mixed = jnp.einsum("tk,tkd->td", gates, values.astype(jnp.float32))
    return mixed.astype(jnp.bfloat16)


def moe_kernel(
    Z, Q, G, tok, router, ids, w_gate, w_up, w_down, out,
    rows, ids_v, router_v, gate_v, up_v, down_v, act,
    keep, core_out, core_in, y_out, y_in, z_out, z_in,
    load_sem, gz_s, gz_r, gy_s, gy_r, gc_s, gc_r,
    rc_s, rc_r, ry_s, ry_r, rz_s, rz_r,
):
    R, D = tok.shape
    experts = router.shape[0]
    ff = gate_v.shape[1]
    half, quarter = 2 * Z * R, Z * R
    cols = D // Q
    me = lax.axis_index("exp")
    core, y, z = lax.rem(me, 2), lax.rem(me // 2, 2), me // 4
    core_peer = {"exp": me + 1 - 2 * core}
    y_peer = {"exp": me + 2 - 4 * y}

    def z_peer(shift):
        return {"exp": lax.rem(z + shift, Z) * 4 + 2 * y + core}

    def remote(src, dst, send, recv, peer):
        return pltpu.make_async_remote_copy(
            src_ref=src, dst_ref=dst, send_sem=send, recv_sem=recv,
            device_id=peer, device_id_type=MESH,
        )

    loads = [
        pltpu.make_async_copy(ids, ids_v, load_sem.at[0]),
        pltpu.make_async_copy(tok, rows.at[pl.ds(0, R), pl.ds(0, D)], load_sem.at[1]),
        pltpu.make_async_copy(router, router_v, load_sem.at[2]),
        pltpu.make_async_copy(w_gate.at[0], gate_v, load_sem.at[3]),
        pltpu.make_async_copy(w_up.at[0], up_v, load_sem.at[4]),
        pltpu.make_async_copy(w_down.at[0], down_v, load_sem.at[5]),
    ]
    for load in loads[:2]:
        load.start()
    barrier = pltpu.get_barrier_semaphore()
    for peer in [core_peer, y_peer] + [z_peer(s) for s in range(1, Z)]:
        pl.semaphore_signal(barrier, inc=1, device_id=peer, device_id_type=MESH)
    for load in loads[2:]:
        load.start()
    loads[0].wait()
    lane = lax.broadcasted_iota(jnp.int32, (LANES, R), 0)
    named = jnp.zeros((LANES, R), jnp.float32)
    for k in range(ids.shape[0]):
        named = jnp.where(ids_v[k : k + 1, :] == lane, 1.0, named)
    rows[0:R, D : D + LANES] = named.T.astype(jnp.bfloat16)
    loads[1].wait()
    pl.semaphore_wait(barrier, Z + 1)

    tiles = rows.shape[1] // LANES
    edges = [(tiles * g + G - 1) // G * LANES for g in range(G + 1)]

    def slots(i, n, g):
        return rows.at[pl.ds(i * R, n * R), pl.ds(edges[g], edges[g + 1] - edges[g])]

    along_z = [
        [remote(slots(0, 1, g), slots(s, 1, g), gz_s.at[g, s], gz_r.at[g, s], z_peer(Z - s)) for s in range(Z)]
        for g in range(G)
    ]
    across_y = [
        [remote(slots(s, 1, g), slots(2 * Z + s, 1, g), gy_s.at[g, s], gy_r.at[g, s], y_peer) for s in range(Z)]
        for g in range(G)
    ]
    to_core = [
        [
            remote(slots(2 * h * Z, Z, g), slots((2 * h + 1) * Z, Z, g), gc_s.at[g, h], gc_r.at[g, h], core_peer)
            for h in range(2)
        ]
        for g in range(G)
    ]
    order = sorted(range(1, Z), key=lambda s: min(s, Z - s))
    for g in range(G):
        across_y[g][0].start()
        for s in order:
            along_z[g][s].start()
    for g in range(G):
        for s in order:
            along_z[g][s].wait_recv()
            across_y[g][s].start()
        to_core[g][0].start()

    def hidden(h):
        mine = slice(h * half, (h + 1) * half)
        logits = lax.dot_general(
            rows[mine, 0:D], router_v[...], (((1,), (1,)), ((), ())), preferred_element_type=jnp.float32
        )
        chosen = rows[mine, D : D + experts].astype(jnp.float32) > 0.5
        top = jnp.max(jnp.where(chosen, logits, -jnp.inf), axis=1, keepdims=True)
        weight = jnp.where(chosen, jnp.exp(jnp.where(chosen, logits - top, 0.0)), 0.0)
        own = lax.broadcasted_iota(jnp.int32, weight.shape, 1) == me
        share = jnp.sum(jnp.where(own, weight, 0.0), axis=1, keepdims=True)
        step = 256
        for j in range(0, ff, step):
            g = jnp.dot(rows[mine, 0:D], gate_v[:, j : j + step], preferred_element_type=jnp.float32)
            u = jnp.dot(rows[mine, 0:D], up_v[:, j : j + step], preferred_element_type=jnp.float32)
            act[mine, j : j + step] = (g / (1.0 + jnp.exp(-g)) * u).astype(jnp.bfloat16)
        return share / jnp.sum(weight, axis=1, keepdims=True)

    for g in range(G):
        to_core[g][0].wait_recv()
    for load in loads[2:]:
        load.wait()
    gates = [hidden(0)]
    for g in range(G):
        for s in [0] + order:
            across_y[g][s].wait_recv()
        to_core[g][1].start()
    for g in range(G):
        to_core[g][1].wait_recv()
    gates.append(hidden(1))

    core_back = [
        [remote(core_out.at[h, q], core_in.at[h, q], rc_s.at[h, q], rc_r.at[h, q], core_peer) for q in range(Q)]
        for h in range(2)
    ]
    y_back = [remote(y_out.at[q], y_in.at[q], ry_s.at[q], ry_r.at[q], y_peer) for q in range(Q)]
    z_back = [
        [
            remote(z_out.at[q, s - 1], z_in.at[q, s - 1], rz_s.at[q, s - 1], rz_r.at[q, s - 1], z_peer(s))
            for s in range(1, Z)
        ]
        for q in range(Q)
    ]

    def first(h, q):
        o = jnp.dot(
            act[h * half : (h + 1) * half], down_v[:, q * cols : (q + 1) * cols],
            preferred_element_type=jnp.float32,
        )
        o = o * gates[h]
        core_out[h, q] = o[quarter:].astype(jnp.bfloat16)
        keep[h, q] = o[:quarter]
        core_back[h][q].start()

    def second(q):
        core_back[1][q].wait_recv()
        y_out[q] = (keep[1, q] + core_in[1, q].astype(jnp.float32)).astype(jnp.bfloat16)
        y_back[q].start()

    def third(q):
        core_back[0][q].wait_recv()
        y_back[q].wait_recv()
        total = keep[0, q] + core_in[0, q].astype(jnp.float32) + y_in[q].astype(jnp.float32)
        for s in range(1, Z):
            z_out[q, s - 1] = total[s * R : (s + 1) * R].astype(jnp.bfloat16)
            z_back[q][s - 1].start()
        keep[0, q, 0:R] = total[:R]

    def last(q):
        total = keep[0, q, 0:R]
        for s in range(1, Z):
            z_back[q][s - 1].wait_recv()
            total = total + z_in[q, s - 1].astype(jnp.float32)
        out[:, q * cols : (q + 1) * cols] = total.astype(jnp.bfloat16)

    for q in range(Q):
        first(1, q)
    for q in range(Q):
        second(q)
        first(0, q)
    for stage in (third, last):
        for q in range(Q):
            stage(q)
    sent = [copy for g in range(G) for copy in along_z[g][1:] + across_y[g] + to_core[g]]
    for copy in sent + sum(core_back, []) + y_back + sum(z_back, []):
        copy.wait_send()


def gather_plan(tokens, router_weight, w_gate, w_up, w_down, expert_ids):
    devices = lax.axis_size("exp")
    R, D = tokens.shape
    Z, Q, G = devices // 4, 4, 2
    experts = router_weight.shape[1]
    ff = w_gate.shape[2]
    total, half, quarter, cols = devices * R, devices * R // 2, devices * R // 4, D // Q
    bf, f32, dma = jnp.bfloat16, jnp.float32, pltpu.SemaphoreType.DMA
    return pl.pallas_call(
        functools.partial(moe_kernel, Z, Q, G),
        out_shape=jax.ShapeDtypeStruct((R, D), bf),
        in_specs=[pl.BlockSpec(memory_space=pltpu.HBM)] * 6,
        out_specs=pl.BlockSpec(memory_space=pltpu.VMEM),
        scratch_shapes=[
            pltpu.VMEM((total, D + LANES), bf),
            pltpu.VMEM(expert_ids.shape[::-1], jnp.int32),
            pltpu.VMEM((experts, D), bf),
            pltpu.VMEM((D, ff), bf),
            pltpu.VMEM((D, ff), bf),
            pltpu.VMEM((ff, D), bf),
            pltpu.VMEM((total, ff), bf),
            pltpu.VMEM((2, Q, quarter, cols), f32),
            pltpu.VMEM((2, Q, quarter, cols), bf),
            pltpu.VMEM((2, Q, quarter, cols), bf),
            pltpu.VMEM((Q, quarter, cols), bf),
            pltpu.VMEM((Q, quarter, cols), bf),
            pltpu.VMEM((Q, Z - 1, R, cols), bf),
            pltpu.VMEM((Q, Z - 1, R, cols), bf),
            dma((6,)),
            dma((G, Z)), dma((G, Z)), dma((G, Z)), dma((G, Z)), dma((G, 2)), dma((G, 2)),
            dma((2, Q)), dma((2, Q)), dma((Q,)), dma((Q,)), dma((Q, Z - 1)), dma((Q, Z - 1)),
        ],
        compiler_params=pltpu.CompilerParams(
            collective_id=0, has_side_effects=True, vmem_limit_bytes=60 * 1024 * 1024
        ),
    )(tokens, router_weight.T, expert_ids.T, w_gate, w_up, w_down)


def on_device(tokens, router_weight, w_gate, w_up, w_down, expert_ids):
    devices = lax.axis_size("exp")
    tok_rows, chosen = expert_ids.shape
    experts = devices * w_gate.shape[0]
    capacity = min(tok_rows, max(2, (3 * tok_rows * chosen + 2 * experts - 1) // (2 * experts)))
    args = (tokens, router_weight, w_gate, w_up, w_down, expert_ids)
    if tok_rows <= 2 * capacity:
        return gather_plan(*args)
    return dispatch_plan(*args, capacity)


def solution(mesh):
    placed = (
        P(("grp", "exp"), None),
        P(),
        P("exp", None, None),
        P("exp", None, None),
        P("exp", None, None),
        P(("grp", "exp"), None),
    )
    return jax.shard_map(
        on_device, mesh=mesh, in_specs=placed, out_specs=P(("grp", "exp"), None), check_vma=False
    )
```

```python
import functools
import jax
import jax.numpy as jnp
from jax import lax
from jax.experimental import pallas as pl
from jax.experimental.pallas import tpu as pltpu
from jax.sharding import PartitionSpec as P

LANES = 128
MESH = pl.DeviceIdType.MESH


def expert_rows(rows, gate_mat, up_mat, down_mat):
    gate = jnp.dot(rows, gate_mat, preferred_element_type=jnp.float32)
    upper = jnp.dot(rows, up_mat, preferred_element_type=jnp.float32)
    act = (jax.nn.silu(gate) * upper).astype(jnp.bfloat16)
    return jnp.dot(act, down_mat, preferred_element_type=jnp.float32).astype(jnp.bfloat16)


def dispatch_plan(tokens, router_weight, w_gate, w_up, w_down, expert_ids, capacity):
    devices = lax.axis_size("exp")
    tok_rows, chosen = expert_ids.shape
    width = tokens.shape[1]
    experts = devices * w_gate.shape[0]
    logits = jnp.dot(tokens, router_weight, preferred_element_type=jnp.float32)
    picked = jnp.take_along_axis(logits, expert_ids, axis=1)
    gates = jax.nn.softmax(picked, axis=1)
    flat_ids = expert_ids.reshape(-1)
    onehot = (flat_ids[:, None] == jnp.arange(experts, dtype=jnp.int32)[None, :]).astype(jnp.int32)
    ranks = jnp.cumsum(onehot, axis=0) - onehot
    slot = jnp.sum(ranks * onehot, axis=1)
    place = slot * experts + flat_ids
    repeated = jnp.repeat(tokens, chosen, axis=0)
    filled = jnp.zeros((capacity * experts, width), jnp.bfloat16).at[place].set(repeated)
    received = lax.all_to_all(
        filled.reshape(capacity, experts, width), "exp", split_axis=1, concat_axis=1, tiled=True
    )
    count = received.shape[0]
    outs = expert_rows(received.reshape(-1, width), w_gate[0], w_up[0], w_down[0])
    back = lax.all_to_all(
        outs.reshape(count, experts, width), "exp", split_axis=1, concat_axis=1, tiled=True
    )
    values = back.reshape(capacity * experts, width)[place].reshape(tok_rows, chosen, width)
    mixed = jnp.einsum("tk,tkd->td", gates, values.astype(jnp.float32))
    return mixed.astype(jnp.bfloat16)


def moe_kernel(
    Z, Q, G, tok, router, ids, w_gate, w_up, w_down, out,
    rows, ids_v, router_v, gate_v, up_v, down_v, act,
    keep, core_out, core_in, y_out, y_in, z_out, z_in,
    load_sem, gz_s, gz_r, gy_s, gy_r, gc_s, gc_r,
    rc_s, rc_r, ry_s, ry_r, rz_s, rz_r,
):
    R, D = tok.shape
    experts = router.shape[0]
    ff = gate_v.shape[1]
    half, quarter = 2 * Z * R, Z * R
    cols = D // Q
    me = lax.axis_index("exp")
    core, y, z = lax.rem(me, 2), lax.rem(me // 2, 2), me // 4
    core_peer = {"exp": me + 1 - 2 * core}
    y_peer = {"exp": me + 2 - 4 * y}

    def z_peer(shift):
        return {"exp": lax.rem(z + shift, Z) * 4 + 2 * y + core}

    def remote(src, dst, send, recv, peer):
        return pltpu.make_async_remote_copy(
            src_ref=src, dst_ref=dst, send_sem=send, recv_sem=recv,
            device_id=peer, device_id_type=MESH,
        )

    loads = [
        pltpu.make_async_copy(ids, ids_v, load_sem.at[0]),
        pltpu.make_async_copy(tok, rows.at[pl.ds(0, R), pl.ds(0, D)], load_sem.at[1]),
        pltpu.make_async_copy(router, router_v, load_sem.at[2]),
        pltpu.make_async_copy(w_gate.at[0], gate_v, load_sem.at[3]),
        pltpu.make_async_copy(w_up.at[0], up_v, load_sem.at[4]),
        pltpu.make_async_copy(w_down.at[0], down_v, load_sem.at[5]),
    ]
    for load in loads[:2]:
        load.start()
    barrier = pltpu.get_barrier_semaphore()
    for peer in [core_peer, y_peer] + [z_peer(s) for s in range(1, Z)]:
        pl.semaphore_signal(barrier, inc=1, device_id=peer, device_id_type=MESH)
    for load in loads[2:]:
        load.start()
    loads[0].wait()
    lane = lax.broadcasted_iota(jnp.int32, (LANES, R), 0)
    named = jnp.zeros((LANES, R), jnp.float32)
    for k in range(ids.shape[0]):
        named = jnp.where(ids_v[k : k + 1, :] == lane, 1.0, named)
    rows[0:R, D : D + LANES] = named.T.astype(jnp.bfloat16)
    loads[1].wait()
    pl.semaphore_wait(barrier, Z + 1)

    tiles = rows.shape[1] // LANES
    edges = [(tiles * g + G - 1) // G * LANES for g in range(G + 1)]

    def slots(i, n, g):
        return rows.at[pl.ds(i * R, n * R), pl.ds(edges[g], edges[g + 1] - edges[g])]

    along_z = [
        [remote(slots(0, 1, g), slots(s, 1, g), gz_s.at[g, s], gz_r.at[g, s], z_peer(Z - s)) for s in range(Z)]
        for g in range(G)
    ]
    across_y = [
        [remote(slots(s, 1, g), slots(2 * Z + s, 1, g), gy_s.at[g, s], gy_r.at[g, s], y_peer) for s in range(Z)]
        for g in range(G)
    ]
    to_core = [
        [
            remote(slots(2 * h * Z, Z, g), slots((2 * h + 1) * Z, Z, g), gc_s.at[g, h], gc_r.at[g, h], core_peer)
            for h in range(2)
        ]
        for g in range(G)
    ]
    order = sorted(range(1, Z), key=lambda s: min(s, Z - s))
    for g in range(G):
        across_y[g][0].start()
        for s in order:
            along_z[g][s].start()
    for g in range(G):
        for s in order:
            along_z[g][s].wait_recv()
            across_y[g][s].start()
        to_core[g][0].start()

    def hidden(h):
        mine = slice(h * half, (h + 1) * half)
        logits = lax.dot_general(
            rows[mine, 0:D], router_v[...], (((1,), (1,)), ((), ())), preferred_element_type=jnp.float32
        )
        chosen = rows[mine, D : D + experts].astype(jnp.float32) > 0.5
        top = jnp.max(jnp.where(chosen, logits, -jnp.inf), axis=1, keepdims=True)
        weight = jnp.where(chosen, jnp.exp(jnp.where(chosen, logits - top, 0.0)), 0.0)
        own = lax.broadcasted_iota(jnp.int32, weight.shape, 1) == me
        share = jnp.sum(jnp.where(own, weight, 0.0), axis=1, keepdims=True)
        step = 256
        for j in range(0, ff, step):
            g = jnp.dot(rows[mine, 0:D], gate_v[:, j : j + step], preferred_element_type=jnp.float32)
            u = jnp.dot(rows[mine, 0:D], up_v[:, j : j + step], preferred_element_type=jnp.float32)
            act[mine, j : j + step] = (g / (1.0 + jnp.exp(-g)) * u).astype(jnp.bfloat16)
        return share / jnp.sum(weight, axis=1, keepdims=True)

    for g in range(G):
        to_core[g][0].wait_recv()
    for load in loads[2:]:
        load.wait()
    gates = [hidden(0)]
    for g in range(G):
        for s in [0] + order:
            across_y[g][s].wait_recv()
        to_core[g][1].start()
    for g in range(G):
        to_core[g][1].wait_recv()
    gates.append(hidden(1))

    core_back = [
        [remote(core_out.at[h, q], core_in.at[h, q], rc_s.at[h, q], rc_r.at[h, q], core_peer) for q in range(Q)]
        for h in range(2)
    ]
    y_back = [remote(y_out.at[q], y_in.at[q], ry_s.at[q], ry_r.at[q], y_peer) for q in range(Q)]
    z_back = [
        [
            remote(z_out.at[q, s - 1], z_in.at[q, s - 1], rz_s.at[q, s - 1], rz_r.at[q, s - 1], z_peer(s))
            for s in range(1, Z)
        ]
        for q in range(Q)
    ]

    def first(h, q):
        o = jnp.dot(
            act[h * half : (h + 1) * half], down_v[:, q * cols : (q + 1) * cols],
            preferred_element_type=jnp.float32,
        )
        o = o * gates[h]
        core_out[h, q] = o[quarter:].astype(jnp.bfloat16)
        keep[h, q] = o[:quarter]
        core_back[h][q].start()

    def second(q):
        core_back[1][q].wait_recv()
        y_out[q] = (keep[1, q] + core_in[1, q].astype(jnp.float32)).astype(jnp.bfloat16)
        y_back[q].start()

    def third(q):
        core_back[0][q].wait_recv()
        y_back[q].wait_recv()
        total = keep[0, q] + core_in[0, q].astype(jnp.float32) + y_in[q].astype(jnp.float32)
        for s in range(1, Z):
            z_out[q, s - 1] = total[s * R : (s + 1) * R].astype(jnp.bfloat16)
            z_back[q][s - 1].start()
        keep[0, q, 0:R] = total[:R]

    def last(q):
        total = keep[0, q, 0:R]
        for s in range(1, Z):
            z_back[q][s - 1].wait_recv()
            total = total + z_in[q, s - 1].astype(jnp.float32)
        out[:, q * cols : (q + 1) * cols] = total.astype(jnp.bfloat16)

    for q in range(Q):
        first(1, q)
    for q in range(Q):
        second(q)
        first(0, q)
    for stage in (third, last):
        for q in range(Q):
            stage(q)
    sent = [copy for g in range(G) for copy in along_z[g][1:] + across_y[g] + to_core[g]]
    for copy in sent + sum(core_back, []) + y_back + sum(z_back, []):
        copy.wait_send()


def gather_plan(tokens, router_weight, w_gate, w_up, w_down, expert_ids):
    devices = lax.axis_size("exp")
    R, D = tokens.shape
    Z, Q, G = devices // 4, 4, 1
    experts = router_weight.shape[1]
    ff = w_gate.shape[2]
    total, half, quarter, cols = devices * R, devices * R // 2, devices * R // 4, D // Q
    bf, f32, dma = jnp.bfloat16, jnp.float32, pltpu.SemaphoreType.DMA
    return pl.pallas_call(
        functools.partial(moe_kernel, Z, Q, G),
        out_shape=jax.ShapeDtypeStruct((R, D), bf),
        in_specs=[pl.BlockSpec(memory_space=pltpu.HBM)] * 6,
        out_specs=pl.BlockSpec(memory_space=pltpu.VMEM),
        scratch_shapes=[
            pltpu.VMEM((total, D + LANES), bf),
            pltpu.VMEM(expert_ids.shape[::-1], jnp.int32),
            pltpu.VMEM((experts, D), bf),
            pltpu.VMEM((D, ff), bf),
            pltpu.VMEM((D, ff), bf),
            pltpu.VMEM((ff, D), bf),
            pltpu.VMEM((total, ff), bf),
            pltpu.VMEM((2, Q, quarter, cols), f32),
            pltpu.VMEM((2, Q, quarter, cols), bf),
            pltpu.VMEM((2, Q, quarter, cols), bf),
            pltpu.VMEM((Q, quarter, cols), bf),
            pltpu.VMEM((Q, quarter, cols), bf),
            pltpu.VMEM((Q, Z - 1, R, cols), bf),
            pltpu.VMEM((Q, Z - 1, R, cols), bf),
            dma((6,)),
            dma((G, Z)), dma((G, Z)), dma((G, Z)), dma((G, Z)), dma((G, 2)), dma((G, 2)),
            dma((2, Q)), dma((2, Q)), dma((Q,)), dma((Q,)), dma((Q, Z - 1)), dma((Q, Z - 1)),
        ],
        compiler_params=pltpu.CompilerParams(
            collective_id=0, has_side_effects=True, vmem_limit_bytes=60 * 1024 * 1024
        ),
    )(tokens, router_weight.T, expert_ids.T, w_gate, w_up, w_down)


def on_device(tokens, router_weight, w_gate, w_up, w_down, expert_ids):
    devices = lax.axis_size("exp")
    tok_rows, chosen = expert_ids.shape
    experts = devices * w_gate.shape[0]
    capacity = min(tok_rows, max(2, (3 * tok_rows * chosen + 2 * experts - 1) // (2 * experts)))
    args = (tokens, router_weight, w_gate, w_up, w_down, expert_ids)
    if tok_rows <= 2 * capacity:
        return gather_plan(*args)
    return dispatch_plan(*args, capacity)


def solution(mesh):
    placed = (
        P(("grp", "exp"), None),
        P(),
        P("exp", None, None),
        P("exp", None, None),
        P("exp", None, None),
        P(("grp", "exp"), None),
    )
    return jax.shard_map(
        on_device, mesh=mesh, in_specs=placed, out_specs=P(("grp", "exp"), None), check_vma=False
    )
```
